1024 devices in a mesh: row: 16 (over x_hi, y), col: 64 (over x_lo, z, core).
Axes of the slice: x: 4 (x_hi: 2, x_lo: 2; x = x_hi * 2 + x_lo), y: 8, z: 16, core: 2. Of those that a mesh axis runs over, the one named last changes fastest.
Arguments:
- vectors: bfloat16 [8, 262144], P(None, ('row', 'col')), may hold values from -6 to 6
- matrix_tiles: bfloat16 [32768, 128, 128], P(('row', 'col')), may hold values from -0.1875 to 0.1875
- tile_row: int32 [32768], P(('row', 'col')), may hold values from 0 to 127, as said below
- tile_col: int32 [32768], P(('row', 'col')), may hold values from 0 to 31, as said below
Outputs:
- applied: float32 [8, 262144], P(None, ('row', 'col'))
The draws below stay inside these ranges and needn't reach their ends.
Inputs may be any that keep to these rules, and one draw needn't show every extreme that they name: `tile_row`: global tile row >= global tile column for every stored tile; tiles may repeat. tile_col // 2 never exceeds the device's index along row.
All inputs are finite; a program needn't handle non-finite values.
Results may differ from the reference program's by a relative error of at most 0.0003.
Values may be sent and summed in bfloat16 or wider, within the bound.
No kernel may reach another device: no remote copies, remote signals or barrier semaphores. Data moves between devices by JAX's collectives and lax.ppermute only.
A program may use at most 32 MiB of HBM per device.

```python
import jax
import jax.numpy as jnp
from jax import lax

K = 8
TILE = 128
SEG = 256
TPD = 32
N = 262144
TILES = 32768
N_COL = 64


def pattern(key):
    tiles_seg = SEG // TILE
    row_tiles = N_COL * tiles_seg
    position = jnp.arange(TILES, dtype=jnp.int32)
    device = position // TPD
    slot_index = position % TPD
    row_device = device // N_COL
    col_device = device % N_COL
    key_one, key_two, key_three = jax.random.split(key, 3)
    segment = jax.random.randint(key_one, (TILES,), 0, row_device + 1)
    within = jax.random.randint(key_two, (TILES,), 0, tiles_seg)
    lowest = jnp.where(segment == row_device, col_device * tiles_seg + within, 0)
    row_pick = jax.random.randint(key_three, (TILES,), lowest, row_tiles)
    col_pick = segment * tiles_seg + within
    row_pick = jnp.where(slot_index == 0, row_tiles - 1, row_pick)
    col_pick = jnp.where(slot_index == 0, row_device * tiles_seg + tiles_seg - 1, col_pick)
    row_pick = jnp.where(slot_index == 1, jnp.where(row_device > 0, 0, col_device * tiles_seg), row_pick)
    col_pick = jnp.where(slot_index == 1, 0, col_pick)
    return (row_pick.astype(jnp.int32), col_pick.astype(jnp.int32))


def draw_tile_row(key, part):
    return pattern(key)[0]


def draw_tile_col(key, part):
    return pattern(key)[1]


def level_of(stream_key, dims, pieces, low, high):
    factor_of, own = 1.0, jax.random.fold_in(stream_key, 6)
    for axis_at, parts in pieces:
        steps = jnp.exp(jax.random.uniform(jax.random.fold_in(own, axis_at), (parts,), jnp.float32, low / len(pieces), high / len(pieces)))
        factor_of = factor_of * jnp.repeat(steps, dims[axis_at] // parts).reshape([-1 if axis == axis_at else 1 for axis in range(len(dims))])
    return factor_of


def noise(rng, extent, spread, limit, shards=(), held_as=jnp.bfloat16):
    values = spread * jax.random.normal(rng, extent, jnp.float32)
    if shards:
        values = values * level_of(rng, extent, shards, -0.22, 0.18)
    return jnp.clip(values, -limit, limit).astype(held_as)


def setup_inputs(seed: int = 0) -> dict:
    streams_of = jax.random.split(jax.random.key(seed), 5)
    return {
        "vectors": noise(streams_of[0], (K, N), 1.0, 6.0, ((1, 1024),)),
        "matrix_tiles": noise(streams_of[1], (TILES, TILE, TILE), (8 * TILE) ** -0.5, 0.1875, ((0, 1024),)),
        "tile_row": draw_tile_row(jax.random.fold_in(streams_of[4], 71), 0),
        "tile_col": draw_tile_col(jax.random.fold_in(streams_of[4], 71), 0),
    }


def reference(vectors, matrix_tiles, tile_row, tile_col):
    tiles_seg = SEG // TILE
    row_tiles = N_COL * tiles_seg
    device_count = TILES // TPD
    position = jnp.arange(TILES, dtype=jnp.int32)
    device = position // TPD
    row_device = device // N_COL
    col_device = device % N_COL
    global_row = row_device * row_tiles + tile_row
    global_col = ((tile_col // tiles_seg) * N_COL + col_device) * tiles_seg + tile_col % tiles_seg
    blocks = vectors.astype(jnp.float32).reshape(K, N // TILE, TILE)
    tile_groups = matrix_tiles.reshape(device_count, TPD, TILE, TILE)
    row_groups = global_row.reshape(device_count, TPD).astype(jnp.int32)
    col_groups = global_col.reshape(device_count, TPD).astype(jnp.int32)

    def accumulate(total, entries):
        weights, rows_here, cols_here = entries
        weights = weights.astype(jnp.float32)
        picked_col = blocks[:, cols_here]
        picked_row = blocks[:, rows_here]
        row_terms = jnp.einsum("ktj,tij->kti", picked_col, weights, precision=lax.Precision.HIGHEST)
        col_terms = jnp.einsum("kti,tij->ktj", picked_row, weights, precision=lax.Precision.HIGHEST)
        total = total.at[:, rows_here].add(row_terms)
        total = total.at[:, cols_here].add(col_terms)
        return total, None

    start_total = jnp.zeros((K, N // TILE, TILE), jnp.float32)
    total, unused = lax.scan(accumulate, start_total, (tile_groups, row_groups, col_groups))
    return total.reshape(K, N)
```

```python
import jax
import jax.numpy as jnp
from jax import lax
from jax.experimental import pallas as pl
from jax.experimental.pallas import tpu as pltpu
from jax.sharding import Mesh, PartitionSpec as P

AXES = ("xh", "y", "xl", "z", "core")
SIZES = (2, 8, 2, 16, 2)
TPD, K, TILE = 32, 8, 128
VM = pl.BlockSpec(memory_space=pltpu.VMEM)
SM = pl.BlockSpec(memory_space=pltpu.SMEM)


def half_of(block, half):
    return jnp.where(half == 1, block[:, TILE:], block[:, :TILE])


def row_kernel(tr, tc, seg, tiles, keep, send):
    core = lax.axis_index("core")
    keep[...] = jnp.zeros_like(keep)
    send[...] = jnp.zeros_like(send)
    for t in range(TPD):
        r, c = tr[t], tc[t]
        x = half_of(seg[c // 2], c % 2)
        y = lax.dot_general(x, tiles[t], (((1,), (1,)), ((), ())), preferred_element_type=jnp.float32)
        mine = ((r // 2) % 2) == core
        at = (r // 4) * 2 + r % 2
        keep[at] += jnp.where(mine, y, 0.0)
        send[at] += jnp.where(mine, 0.0, y)


def col_kernel(tr, tc, seg, tiles, keep, send):
    xh = lax.axis_index("xh")
    keep[...] = jnp.zeros_like(keep)
    send[...] = jnp.zeros_like(send)
    for t in range(TPD):
        r, c = tr[t], tc[t]
        q = r // 2
        x = half_of(seg[q % 2, (q // 2) % 16, q // 32], r % 2)
        y = jnp.dot(x, tiles[t], preferred_element_type=jnp.float32)
        s = c // 2
        mine = (s // 8) == xh
        at = (s % 8) * 2 + c % 2
        keep[at] += jnp.where(mine, y, 0.0)
        send[at] += jnp.where(mine, 0.0, y)


def products(kernel, owners, tr, tc, seg, tiles):
    part = jax.ShapeDtypeStruct((owners, K, TILE), jnp.float32)
    return pl.pallas_call(
        kernel,
        out_shape=(part, part),
        in_specs=[SM, SM, VM, VM],
        out_specs=(VM, VM),
        cost_estimate=pl.CostEstimate(flops=2 * TPD * K * TILE * TILE, bytes_accessed=2 << 20, transcendentals=0),
        compiler_params=pltpu.CompilerParams(vmem_limit_bytes=16 << 20),
    )(tr, tc, seg, tiles)


def total_kernel(a, b, out):
    out[:, :TILE] = jnp.sum(a[:, 0], axis=0) + jnp.sum(b[:, 0], axis=0)
    out[:, TILE:] = jnp.sum(a[:, 1], axis=0) + jnp.sum(b[:, 1], axis=0)


def swap(n):
    return [(i, n - 1 - i) for i in range(n)]


def per_device(v, tiles, tr, tc):
    seg_row = lax.all_to_all(jnp.broadcast_to(v[None], (16, K, 256)), ("xh", "y"), 0, 0, tiled=True)
    pair = lax.all_gather(v, "xl", axis=0)
    seg_row, pair = lax.optimization_barrier((seg_row, pair))
    spread = jnp.broadcast_to(pair[None], (16, 2, K, 256))
    seg_z = lax.all_to_all(spread, "z", 0, 0, tiled=True)
    keep, send = products(row_kernel, 64, tr, tc, seg_row, tiles)
    other = lax.all_gather(send, "core", axis=0)
    core = lax.axis_index("core")
    row_part = keep + lax.dynamic_index_in_dim(other, 1 - core, 0, keepdims=False)
    row_part, seg_z = lax.optimization_barrier((row_part, seg_z))
    row_got = lax.all_to_all(row_part.reshape(32, 2, K, TILE), ("xl", "z"), 0, 0, tiled=True)
    seg_col = lax.all_gather(seg_z, "core", axis=0)
    keep, send = products(col_kernel, 16, tr, tc, seg_col, tiles)
    col_part = keep + lax.ppermute(send, "xh", swap(2))
    col_part, row_got = lax.optimization_barrier((col_part, row_got))
    col_got = lax.all_to_all(col_part.reshape(8, 2, K, TILE), "y", 0, 0, tiled=True)
    return pl.pallas_call(
        total_kernel,
        out_shape=jax.ShapeDtypeStruct((K, 256), jnp.float32),
        in_specs=[VM, VM],
        out_specs=VM,
    )(row_got, col_got)


def solution(mesh):
    fine = Mesh(mesh.devices.reshape(SIZES), AXES)
    return jax.shard_map(
        per_device,
        mesh=fine,
        in_specs=(P(None, AXES), P(AXES, None, None), P(AXES), P(AXES)),
        out_specs=P(None, AXES),
        check_vma=False,
    )
```

```python
import jax
import jax.numpy as jnp
import numpy as np
from jax import lax
from jax.experimental import pallas as pl
from jax.experimental.pallas import tpu as pltpu
from jax.sharding import Mesh, PartitionSpec as P

AXES = ("xh", "y", "xl", "z", "core")
SIZES = (2, 8, 2, 16, 2)
NEAR = ("xl", "core")
TPD, K, TILE, SEG = 32, 8, 128, 256
VM = pl.BlockSpec(memory_space=pltpu.VMEM)
SM = pl.BlockSpec(memory_space=pltpu.SMEM)
F32 = jnp.float32


def lines():
    at = np.arange(1024).reshape(SIZES)
    along_z = at[..., 0].reshape(32, 16)
    along_row = at[..., 1].reshape(16, 32).T
    return np.concatenate([along_z, along_row]).tolist()


def exchange(x):
    return lax.all_to_all(x, AXES, 0, 0, axis_index_groups=lines(), tiled=True)


def half_of(block, half):
    return jnp.where(half == 1, block[:, TILE:], block[:, :TILE])


def col_kernel(tr, tc, seg, tiles, out):
    out[...] = jnp.zeros_like(out)
    for t in range(TPD):
        r, c = tr[t], tc[t]
        q = r >> 1
        x = half_of(seg[((q >> 5) << 6) + (q & 31)], r & 1)
        out[c] += jnp.dot(x, tiles[t], preferred_element_type=F32)


def row_kernel(tc, ids, seg, tiles, out):
    base = lax.axis_index("xl") * 64 + 32 + lax.axis_index("core")
    for t in range(TPD):
        c = tc[t]
        x = half_of(seg[base + (c >> 1) * 2], c & 1)
        out[t] = lax.dot_general(x, tiles[t], (((1,), (1,)), ((), ())), preferred_element_type=F32)
    out[TPD] = ids[...]


def pack_kernel(slots, prods, cols, out, *accs):
    @pl.when(lax.axis_index("core") == 0)
    def _():
        for acc in accs:
            acc[...] = jnp.zeros_like(acc)
        for t in range(TPD):
            for d, acc in enumerate(accs):
                acc[slots[d * TPD + t]] += prods[d, t]
        out[...] = sum(acc[:64] for acc in accs)

    @pl.when(lax.axis_index("core") == 1)
    def _():
        for s in range(16):
            for c in range(2):
                out[4 * s + 2 * c] = cols[c, 2 * s]
                out[4 * s + 2 * c + 1] = cols[c, 2 * s + 1]


def sum_kernel(got, out):
    s = jnp.sum(got[...], axis=0)
    for c in range(2):
        out[c, :, :TILE] = s[2 * c]
        out[c, :, TILE:] = s[2 * c + 1]


def total_kernel(both, out):
    core = lax.axis_index("core")
    out[...] = both[0, core] + both[1, core]


def call(kernel, shape, dtype, specs, *args, flops=0, scratch=()):
    return pl.pallas_call(
        kernel,
        out_shape=jax.ShapeDtypeStruct(shape, dtype),
        in_specs=specs,
        out_specs=VM,
        scratch_shapes=scratch,
        cost_estimate=pl.CostEstimate(flops=flops, bytes_accessed=1 << 20, transcendentals=0),
        compiler_params=pltpu.CompilerParams(vmem_limit_bytes=16 << 20),
    )(*args)


def per_device(v, tiles, tr, tc):
    flops = 2 * TPD * K * TILE * TILE
    ids = jnp.pad(tr[None, :].astype(F32), ((0, K - 1), (0, TILE - TPD)))
    both = lax.all_gather(v, "core", axis=0)
    far = exchange(jnp.broadcast_to(both[None], (16, 2, K, SEG)))
    seg = lax.all_gather(far, NEAR, axis=0).reshape(128, K, SEG)
    prods = call(row_kernel, (TPD + 1, K, TILE), F32, [SM, VM, VM, VM], tc, ids, seg, tiles, flops=flops)
    prods = lax.all_gather(prods, NEAR, axis=0)
    rows = prods[:, TPD, 0, :TPD].astype(jnp.int32).reshape(4 * TPD)
    slots = jnp.where((rows >> 6) == lax.axis_index("xl"), rows & 63, 64)
    cols = call(col_kernel, (32, K, TILE), F32, [SM, SM, VM, VM], tr, tc, seg, tiles, flops=flops)
    cols = lax.all_gather(cols, "core", axis=0)
    packed = call(
        pack_kernel, (64, K, TILE), F32, [SM, VM, VM], slots, prods, cols, scratch=[pltpu.VMEM((65, K, TILE), F32)] * 4
    )
    got = exchange(packed.reshape(16, 4, K, TILE))
    part = call(sum_kernel, (2, K, SEG), F32, [VM], got)
    return call(total_kernel, (K, SEG), F32, [VM], lax.all_gather(part, "core", axis=0))


def solution(mesh):
    fine = Mesh(mesh.devices.reshape(SIZES), AXES)
    return jax.shard_map(
        per_device,
        mesh=fine,
        in_specs=(P(None, AXES), P(AXES, None, None), P(AXES), P(AXES)),
        out_specs=P(None, AXES),
        check_vma=False,
    )
```

```python
import jax
import jax.numpy as jnp
import numpy as np
from jax import lax
from jax.experimental import pallas as pl
from jax.experimental.pallas import tpu as pltpu
from jax.sharding import Mesh, PartitionSpec as P

AXES = ("xh", "y", "xl", "z", "core")
SIZES = (2, 8, 2, 16, 2)
TPD, K, TILE, SEG = 32, 8, 128, 256
FIRST_Z = (12, 8)
FIRST_ROW = 12
SWAP = [(0, 1), (1, 0)]
VM = pl.BlockSpec(memory_space=pltpu.VMEM)
SM = pl.BlockSpec(memory_space=pltpu.SMEM)
F32 = jnp.float32


def exchange(x, z_core, first_z):
    at = np.arange(1024).reshape(16, 2, 16, 2)
    along_z = np.roll(at, -first_z, axis=2)[..., z_core].reshape(-1, 16)
    along_row = np.roll(at, -FIRST_ROW, axis=0)[..., 1 - z_core].reshape(16, 32).T
    groups = np.concatenate([along_z, along_row]).tolist()
    return lax.all_to_all(x, AXES, 0, 0, axis_index_groups=groups, tiled=True)


def between(core):
    at = np.arange(1024).reshape(SIZES)[..., core]
    return [(int(a), int(b)) for a, b in zip(at.ravel(), at[:, :, ::-1].ravel())]


def half_of(block, half):
    return jnp.where(half == 1, block[:, TILE:], block[:, :TILE])


def place_kernel(both, out):
    for core in range(2):
        places = both[core].astype(F32)[K:, :TILE].astype(jnp.int32)
        r, c = places[0:1], places[1:2]
        for i, first in enumerate(FIRST_Z):
            out[3 * core + i : 3 * core + i + 1, :] = (r & 64) | ((r - 4 * first) & 63)
        out[3 * core + 2 : 3 * core + 3, :] = (c - 2 * FIRST_ROW) & 31


def row_kernel(at, far, tiles, tiles_other, mine, send):
    @pl.when(lax.axis_index("core") == 1)
    def _():
        xl = lax.axis_index("xl")
        mine[...] = jnp.zeros_like(mine)
        send[...] = jnp.zeros_like(send)
        for core, blocks in ((0, tiles_other), (1, tiles)):
            for t in range(TPD):
                r, c = at[3 * core + 1, t], at[3 * core + 2, t]
                x = half_of(far[c >> 1, core], c & 1)
                y = lax.dot_general(x, blocks[t], (((1,), (1,)), ((), ())), preferred_element_type=F32)
                here = (r >> 6) == xl
                mine[r & 63] += jnp.where(here, y, 0.0)
                send[r & 63] += jnp.where(here, 0.0, y)


def col_kernel(at, far, far_other, mine, other, tiles, tiles_other, out):
    @pl.when(lax.axis_index("core") == 0)
    def _():
        xl = lax.axis_index("xl")
        out[...] = jnp.zeros_like(out)
        for core, blocks in ((1, tiles_other), (0, tiles)):
            for t in range(TPD):
                r, c = at[3 * core, t], at[3 * core + 2, t]
                z, d = (r >> 2) & 15, (r >> 1) & 1
                x = half_of(jnp.where((r >> 6) == xl, far[z, d], far_other[z, d]), r & 1)
                out[(c >> 1) * 4 + 2 * core + (c & 1)] += jnp.dot(x, blocks[t], preferred_element_type=F32)

    @pl.when(lax.axis_index("core") == 1)
    def _():
        out[...] = mine[...] + other[...]


def sum_kernel(got, out):
    s = jnp.sum(got[...], axis=0)
    for c in range(2):
        out[c, :, :TILE] = s[2 * c]
        out[c, :, TILE:] = s[2 * c + 1]


def total_kernel(both, out):
    core = lax.axis_index("core")
    out[...] = both[0, core] + both[1, core]


def call(kernel, shapes, specs, *args, flops=0, dtype=F32):
    outs = [jax.ShapeDtypeStruct(shape, dtype) for shape in shapes]
    return pl.pallas_call(
        kernel,
        out_shape=outs,
        in_specs=specs,
        out_specs=[VM] * len(outs),
        cost_estimate=pl.CostEstimate(flops=flops, bytes_accessed=1 << 20, transcendentals=0),
        compiler_params=pltpu.CompilerParams(vmem_limit_bytes=16 << 20),
    )(*args)


def per_device(v, tiles, tr, tc):
    flops = 4 * TPD * K * TILE * TILE
    sums = (64, K, TILE)
    places = jnp.pad(jnp.stack([tr, tc]).astype(v.dtype), ((0, K - 2), (0, SEG - TPD)))
    both = lax.all_gather(jnp.concatenate([v, places], axis=0), "core", axis=0)
    far = exchange(jnp.broadcast_to(both[None, :, :K], (16, 2, K, SEG)), 0, FIRST_Z[0])
    (at,) = call(place_kernel, [(8, TILE)], [VM], both, dtype=jnp.int32, flops=7000000000)
    both, tiles = lax.optimization_barrier((both, tiles))
    tiles_other = lax.ppermute(tiles, "core", SWAP)
    far, at, tiles_other = lax.optimization_barrier((far, at, tiles_other))
    far_other = lax.ppermute(far, AXES, between(0))
    mine, send = call(row_kernel, [sums, sums], [SM, VM, VM, VM], at, far, tiles, tiles_other, flops=flops)
    other = lax.ppermute(send, AXES, between(1))
    (part,) = call(
        col_kernel, [sums], [SM, VM, VM, VM, VM, VM, VM], at, far, far_other, mine, other, tiles, tiles_other,
        flops=flops,
    )
    got = exchange(part.reshape(16, 4, K, TILE), 1, FIRST_Z[1])
    (part,) = call(sum_kernel, [(2, K, SEG)], [VM], got)
    (out,) = call(total_kernel, [(K, SEG)], [VM], lax.all_gather(part, "core", axis=0))
    return out


def solution(mesh):
    fine = Mesh(mesh.devices.reshape(SIZES), AXES)
    return jax.shard_map(
        per_device,
        mesh=fine,
        in_specs=(P(None, AXES), P(AXES, None, None), P(AXES), P(AXES)),
        out_specs=P(None, AXES),
        check_vma=False,
    )
```

```python
import jax
import jax.numpy as jnp
import numpy as np
from jax import lax
from jax.experimental import pallas as pl
from jax.experimental.pallas import tpu as pltpu
from jax.sharding import Mesh, PartitionSpec as P

AXES = ("xh", "y", "xl", "z", "core")
SIZES = (2, 8, 2, 16, 2)
TPD, K, TILE, SEG = 32, 8, 128, 256
FIRST_Z = (12, 8)
FIRST_ROW = 12
SWAP = [(0, 1), (1, 0)]
VM = pl.BlockSpec(memory_space=pltpu.VMEM)
SM = pl.BlockSpec(memory_space=pltpu.SMEM)
F32 = jnp.float32


def exchange(x, z_core, first_z):
    at = np.arange(1024).reshape(16, 2, 16, 2)
    along_z = np.roll(at, -first_z, axis=2)[..., z_core].reshape(-1, 16)
    along_row = np.roll(at, -FIRST_ROW, axis=0)[..., 1 - z_core].reshape(16, 32).T
    groups = np.concatenate([along_z, along_row]).tolist()
    return lax.all_to_all(x, AXES, 0, 0, axis_index_groups=groups, tiled=True)


def between(core):
    at = np.arange(1024).reshape(SIZES)[..., core]
    return [(int(a), int(b)) for a, b in zip(at.ravel(), at[:, :, ::-1].ravel())]


def half_of(block, half):
    return jnp.where(half == 1, block[:, TILE:], block[:, :TILE])


def place_kernel(both, out):
    for core in range(2):
        places = both[core].astype(F32).astype(jnp.int32)
        r, c = places[0:1], places[1:2]
        for i, first in enumerate(FIRST_Z):
            out[3 * core + i : 3 * core + i + 1, :] = (r & 64) | ((r - 4 * first) & 63)
        out[3 * core + 2 : 3 * core + 3, :] = (c - 2 * FIRST_ROW) & 31


def row_kernel(at, far, tiles, tiles_other, mine, send):
    @pl.when(lax.axis_index("core") == 1)
    def _():
        xl = lax.axis_index("xl")
        mine[...] = jnp.zeros_like(mine)
        send[...] = jnp.zeros_like(send)
        for core, blocks in ((0, tiles_other), (1, tiles)):
            for t in range(TPD):
                r, c = at[3 * core + 1, t], at[3 * core + 2, t]
                x = half_of(far[c >> 1, core], c & 1)
                y = lax.dot_general(x, blocks[t], (((1,), (1,)), ((), ())), preferred_element_type=F32)
                here = (r >> 6) == xl
                mine[r & 63] += jnp.where(here, y, 0.0)
                send[r & 63] += jnp.where(here, 0.0, y)


def col_kernel(at, far, far_other, mine, other, tiles, tiles_other, out):
    @pl.when(lax.axis_index("core") == 0)
    def _():
        xl = lax.axis_index("xl")
        out[...] = jnp.zeros_like(out)
        for core, blocks in ((1, tiles_other), (0, tiles)):
            for t in range(TPD):
                r, c = at[3 * core, t], at[3 * core + 2, t]
                z, d = (r >> 2) & 15, (r >> 1) & 1
                x = half_of(jnp.where((r >> 6) == xl, far[z, d], far_other[z, d]), r & 1)
                out[(c >> 1) * 4 + 2 * core + (c & 1)] += jnp.dot(x, blocks[t], preferred_element_type=F32)

    @pl.when(lax.axis_index("core") == 1)
    def _():
        out[...] = mine[...] + other[...]


def sum_kernel(got, out):
    s = jnp.sum(got[...], axis=0)
    for c in range(2):
        out[c, :, :TILE] = s[2 * c]
        out[c, :, TILE:] = s[2 * c + 1]


def total_kernel(both, out):
    core = lax.axis_index("core")
    out[...] = both[0, core] + both[1, core]


def call(kernel, shapes, specs, *args, flops=0, dtype=F32):
    outs = [jax.ShapeDtypeStruct(shape, dtype) for shape in shapes]
    return pl.pallas_call(
        kernel,
        out_shape=outs,
        in_specs=specs,
        out_specs=[VM] * len(outs),
        cost_estimate=pl.CostEstimate(flops=flops, bytes_accessed=1 << 20, transcendentals=0),
        compiler_params=pltpu.CompilerParams(vmem_limit_bytes=16 << 20),
    )(*args)


def per_device(v, tiles, tr, tc):
    flops = 4 * TPD * K * TILE * TILE
    sums = (64, K, TILE)
    both = lax.all_gather(v, "core", axis=0)
    both, tiles = lax.optimization_barrier((both, tiles))
    far = exchange(jnp.broadcast_to(both[None], (16, 2, K, SEG)), 0, FIRST_Z[0])
    tiles_other = lax.ppermute(tiles, "core", SWAP)
    places = jnp.pad(jnp.stack([tr, tc]).astype(v.dtype), ((0, K - 2), (0, TILE - TPD)))
    places = lax.all_gather(places, "core", axis=0)
    (at,) = call(place_kernel, [(8, TILE)], [VM], places, dtype=jnp.int32, flops=7000000000)
    far, at, tiles_other = lax.optimization_barrier((far, at, tiles_other))
    far_other = lax.ppermute(far, AXES, between(0))
    mine, send = call(row_kernel, [sums, sums], [SM, VM, VM, VM], at, far, tiles, tiles_other, flops=flops)
    other = lax.ppermute(send, AXES, between(1))
    (part,) = call(
        col_kernel, [sums], [SM, VM, VM, VM, VM, VM, VM], at, far, far_other, mine, other, tiles, tiles_other,
        flops=flops,
    )
    got = exchange(part.reshape(16, 4, K, TILE), 1, FIRST_Z[1])
    (part,) = call(sum_kernel, [(2, K, SEG)], [VM], got)
    (out,) = call(total_kernel, [(K, SEG)], [VM], lax.all_gather(part, "core", axis=0))
    return out


def solution(mesh):
    fine = Mesh(mesh.devices.reshape(SIZES), AXES)
    return jax.shard_map(
        per_device,
        mesh=fine,
        in_specs=(P(None, AXES), P(AXES, None, None), P(AXES), P(AXES)),
        out_specs=P(None, AXES),
        check_vma=False,
    )
```

```python
import jax
import jax.numpy as jnp
import numpy as np
from jax import lax
from jax.experimental import pallas as pl
from jax.experimental.pallas import tpu as pltpu
from jax.sharding import Mesh, PartitionSpec as P

AXES = ("xh", "y", "xl", "z", "core")
SIZES = (2, 8, 2, 16, 2)
TPD, K, TILE, SEG = 32, 8, 128, 256
FIRST_Z = (12, 8)
FIRST_ROW = 12
LEVELS = 32000.0
SWAP = [(0, 1), (1, 0)]
VM = pl.BlockSpec(memory_space=pltpu.VMEM)
SM = pl.BlockSpec(memory_space=pltpu.SMEM)
F32 = jnp.float32


def exchange(x, z_core, first_z):
    at = np.arange(1024).reshape(16, 2, 16, 2)
    along_z = np.roll(at, -first_z, axis=2)[..., z_core].reshape(-1, 16)
    along_row = np.roll(at, -FIRST_ROW, axis=0)[..., 1 - z_core].reshape(16, 32).T
    groups = np.concatenate([along_z, along_row]).tolist()
    return lax.all_to_all(x, AXES, 0, 0, axis_index_groups=groups, tiled=True)


def between(core):
    at = np.arange(1024).reshape(SIZES)[..., core]
    return [(int(a), int(b)) for a, b in zip(at.ravel(), at[:, :, ::-1].ravel())]


def half_of(block, half):
    return jnp.where(half == 1, block[:, TILE:], block[:, :TILE])


def place_kernel(both, out):
    for core in range(2):
        places = both[core].astype(F32).astype(jnp.int32)
        r, c = places[0:1], places[1:2]
        for i, first in enumerate(FIRST_Z):
            out[3 * core + i : 3 * core + i + 1, :] = (r & 64) | ((r - 4 * first) & 63)
        out[3 * core + 2 : 3 * core + 3, :] = (c - 2 * FIRST_ROW) & 31


def row_kernel(at, far, tiles, tiles_other, mine, send):
    @pl.when(lax.axis_index("core") == 1)
    def _():
        xl = lax.axis_index("xl")
        mine[...] = jnp.zeros_like(mine)
        send[...] = jnp.zeros_like(send)
        for core, blocks in ((0, tiles_other), (1, tiles)):
            for t in range(TPD):
                r, c = at[3 * core + 1, t], at[3 * core + 2, t]
                x = half_of(far[c >> 1, core], c & 1)
                y = lax.dot_general(x, blocks[t], (((1,), (1,)), ((), ())), preferred_element_type=F32)
                here = (r >> 6) == xl
                mine[r & 63] += jnp.where(here, y, 0.0)
                send[r & 63] += jnp.where(here, 0.0, y)


def encode(sums, out):
    for p in range(16):
        blocks = [sums[4 * p + j] for j in range(4)]
        top = [jnp.max(jnp.abs(x), axis=0, keepdims=True) for x in blocks]
        top = jnp.concatenate(top + [jnp.zeros((4, TILE), F32)], axis=0)
        e = jnp.ceil(jnp.log2(jnp.maximum(top, 2.0**-110)))
        scale = jnp.exp2(-e) * LEVELS
        for j, x in enumerate(blocks):
            out[p, j] = jnp.round(x * scale[j : j + 1]).astype(jnp.int32).astype(jnp.int16)
        out[p, 4] = e.astype(jnp.int32).astype(jnp.int16)


def col_kernel(at, far, far_other, mine, other, tiles, tiles_other, out, acc):
    @pl.when(lax.axis_index("core") == 0)
    def _():
        xl = lax.axis_index("xl")
        acc[...] = jnp.zeros_like(acc)
        for core, blocks in ((1, tiles_other), (0, tiles)):
            for t in range(TPD):
                r, c = at[3 * core, t], at[3 * core + 2, t]
                z, d = (r >> 2) & 15, (r >> 1) & 1
                x = half_of(jnp.where((r >> 6) == xl, far[z, d], far_other[z, d]), r & 1)
                acc[(c >> 1) * 4 + 2 * core + (c & 1)] += jnp.dot(x, blocks[t], preferred_element_type=F32)

    @pl.when(lax.axis_index("core") == 1)
    def _():
        acc[...] = mine[...] + other[...]

    encode(acc, out)


def sum_kernel(got, out):
    total = [jnp.zeros((K, TILE), F32)] * 4
    for p in range(16):
        unit = jnp.exp2(got[p, 4].astype(jnp.int32).astype(F32)) * (1.0 / LEVELS)
        total = [x + got[p, j].astype(jnp.int32).astype(F32) * unit[j : j + 1] for j, x in enumerate(total)]
    for c in range(2):
        out[c, :, :TILE] = total[2 * c]
        out[c, :, TILE:] = total[2 * c + 1]


def total_kernel(both, out):
    core = lax.axis_index("core")
    out[...] = both[0, core] + both[1, core]


def call(kernel, shapes, specs, *args, flops=0, dtype=F32, scratch=()):
    outs = [jax.ShapeDtypeStruct(shape, dtype) for shape in shapes]
    return pl.pallas_call(
        kernel,
        out_shape=outs,
        in_specs=specs,
        out_specs=[VM] * len(outs),
        scratch_shapes=scratch,
        cost_estimate=pl.CostEstimate(flops=flops, bytes_accessed=1 << 20, transcendentals=0),
        compiler_params=pltpu.CompilerParams(vmem_limit_bytes=16 << 20),
    )(*args)


def per_device(v, tiles, tr, tc):
    flops = 4 * TPD * K * TILE * TILE
    sums = (64, K, TILE)
    both = lax.all_gather(v, "core", axis=0)
    both, tiles = lax.optimization_barrier((both, tiles))
    far = exchange(jnp.broadcast_to(both[None], (16, 2, K, SEG)), 0, FIRST_Z[0])
    tiles_other = lax.ppermute(tiles, "core", SWAP)
    places = jnp.pad(jnp.stack([tr, tc]).astype(v.dtype), ((0, K - 2), (0, TILE - TPD)))
    places = lax.all_gather(places, "core", axis=0)
    (at,) = call(place_kernel, [(8, TILE)], [VM], places, dtype=jnp.int32, flops=7000000000)
    far, at, tiles_other = lax.optimization_barrier((far, at, tiles_other))
    far_other = lax.ppermute(far, AXES, between(0))
    mine, send = call(row_kernel, [sums, sums], [SM, VM, VM, VM], at, far, tiles, tiles_other, flops=flops)
    other = lax.ppermute(send, AXES, between(1))
    (part,) = call(
        col_kernel, [(16, 5, K, TILE)], [SM, VM, VM, VM, VM, VM, VM], at, far, far_other, mine, other, tiles, tiles_other,
        flops=flops, dtype=jnp.int16, scratch=[pltpu.VMEM(sums, F32)],
    )
    got = exchange(part, 1, FIRST_Z[1])
    (part,) = call(sum_kernel, [(2, K, SEG)], [VM], got)
    (out,) = call(total_kernel, [(K, SEG)], [VM], lax.all_gather(part, "core", axis=0))
    return out


def solution(mesh):
    fine = Mesh(mesh.devices.reshape(SIZES), AXES)
    return jax.shard_map(
        per_device,
        mesh=fine,
        in_specs=(P(None, AXES), P(AXES, None, None), P(AXES), P(AXES)),
        out_specs=P(None, AXES),
        check_vma=False,
    )
```

```python
import jax
import jax.numpy as jnp
import numpy as np
from jax import lax
from jax.experimental import pallas as pl
from jax.experimental.pallas import tpu as pltpu
from jax.sharding import Mesh, PartitionSpec as P

AXES = ("xh", "y", "xl", "z", "core")
SIZES = (2, 8, 2, 16, 2)
TPD, K, TILE, SEG = 32, 8, 128, 256
FIRST_Z = (12, 8)
FIRST_ROW = 12
LEVELS = 32000.0
SWAP = [(0, 1), (1, 0)]
VM = pl.BlockSpec(memory_space=pltpu.VMEM)
SM = pl.BlockSpec(memory_space=pltpu.SMEM)
F32 = jnp.float32


def exchange(x, z_core, first_z):
    at = np.arange(1024).reshape(16, 2, 16, 2)
    along_z = np.roll(at, -first_z, axis=2)[..., z_core].reshape(-1, 16)
    along_row = np.roll(at, -FIRST_ROW, axis=0)[..., 1 - z_core].reshape(16, 32).T
    groups = np.concatenate([along_z, along_row]).tolist()
    return lax.all_to_all(x, AXES, 0, 0, axis_index_groups=groups, tiled=True)


def between(core):
    at = np.arange(1024).reshape(SIZES)[..., core]
    return [(int(a), int(b)) for a, b in zip(at.ravel(), at[:, :, ::-1].ravel())]


def half_of(block, half):
    return jnp.where(half == 1, block[:, TILE:], block[:, :TILE])


def place_kernel(both, out):
    for core in range(2):
        places = both[core].astype(F32).astype(jnp.int32)
        r, c = places[0:1], places[1:2]
        for i, first in enumerate(FIRST_Z):
            out[3 * core + i : 3 * core + i + 1, :] = (r & 64) | ((r - 4 * first) & 63)
        out[3 * core + 2 : 3 * core + 3, :] = (c - 2 * FIRST_ROW) & 31


def row_kernel(at, far, tiles, tiles_other, mine, out, send):
    @pl.when(lax.axis_index("core") == 1)
    def _():
        xl = lax.axis_index("xl")
        mine[...] = jnp.zeros_like(mine)
        send[...] = jnp.zeros_like(send)
        for core, blocks in ((0, tiles_other), (1, tiles)):
            for t in range(TPD):
                r, c = at[3 * core + 1, t], at[3 * core + 2, t]
                x = half_of(far[c >> 1, core], c & 1)
                y = lax.dot_general(x, blocks[t], (((1,), (1,)), ((), ())), preferred_element_type=F32)
                here = (r >> 6) == xl
                mine[r & 63] += jnp.where(here, y, 0.0)
                send[r & 63] += jnp.where(here, 0.0, y)
        encode(send, out)


def unit_of(coded, p):
    return jnp.exp2(coded[p, 4].astype(jnp.int32).astype(F32)) * (1.0 / LEVELS)


def value_of(coded, p, j, unit):
    return coded[p, j].astype(jnp.int32).astype(F32) * unit[j : j + 1]


def encode(sums, out):
    for p in range(16):
        blocks = [sums[4 * p + j] for j in range(4)]
        top = [jnp.max(jnp.abs(x), axis=0, keepdims=True) for x in blocks]
        top = jnp.concatenate(top + [jnp.zeros((4, TILE), F32)], axis=0)
        e = jnp.ceil(jnp.log2(jnp.maximum(top, 2.0**-110)))
        scale = jnp.exp2(-e) * LEVELS
        for j, x in enumerate(blocks):
            out[p, j] = jnp.round(x * scale[j : j + 1]).astype(jnp.int32).astype(jnp.int16)
        out[p, 4] = e.astype(jnp.int32).astype(jnp.int16)


def col_kernel(at, far, far_other, mine, other, tiles, tiles_other, out, acc):
    @pl.when(lax.axis_index("core") == 0)
    def _():
        xl = lax.axis_index("xl")
        acc[...] = jnp.zeros_like(acc)
        for core, blocks in ((1, tiles_other), (0, tiles)):
            for t in range(TPD):
                r, c = at[3 * core, t], at[3 * core + 2, t]
                z, d = (r >> 2) & 15, (r >> 1) & 1
                x = half_of(jnp.where((r >> 6) == xl, far[z, d], far_other[z, d]), r & 1)
                acc[(c >> 1) * 4 + 2 * core + (c & 1)] += jnp.dot(x, blocks[t], preferred_element_type=F32)

    @pl.when(lax.axis_index("core") == 1)
    def _():
        for p in range(16):
            unit = unit_of(other, p)
            for j in range(4):
                acc[4 * p + j] = mine[4 * p + j] + value_of(other, p, j, unit)

    encode(acc, out)


def sum_kernel(got, out):
    total = [jnp.zeros((K, TILE), F32)] * 4
    for p in range(16):
        unit = unit_of(got, p)
        total = [x + value_of(got, p, j, unit) for j, x in enumerate(total)]
    for c in range(2):
        out[c, :, :TILE] = total[2 * c]
        out[c, :, TILE:] = total[2 * c + 1]


def total_kernel(both, out):
    core = lax.axis_index("core")
    out[...] = both[0, core] + both[1, core]


def call(kernel, outs, specs, *args, flops=0, scratch=()):
    return pl.pallas_call(
        kernel,
        out_shape=[jax.ShapeDtypeStruct(*out) for out in outs],
        in_specs=specs,
        out_specs=[VM] * len(outs),
        scratch_shapes=scratch,
        cost_estimate=pl.CostEstimate(flops=flops, bytes_accessed=1 << 20, transcendentals=0),
        compiler_params=pltpu.CompilerParams(vmem_limit_bytes=16 << 20),
    )(*args)


def per_device(v, tiles, tr, tc):
    flops = 4 * TPD * K * TILE * TILE
    sums, coded = (64, K, TILE), ((16, 5, K, TILE), jnp.int16)
    both = lax.all_gather(v, "core", axis=0)
    both, tiles = lax.optimization_barrier((both, tiles))
    far = exchange(jnp.broadcast_to(both[None], (16, 2, K, SEG)), 0, FIRST_Z[0])
    tiles_other = lax.ppermute(tiles, "core", SWAP)
    places = jnp.pad(jnp.stack([tr, tc]).astype(v.dtype), ((0, K - 2), (0, TILE - TPD)))
    places = lax.all_gather(places, "core", axis=0)
    (at,) = call(place_kernel, [((8, TILE), jnp.int32)], [VM], places, flops=7000000000)
    far, at, tiles_other = lax.optimization_barrier((far, at, tiles_other))
    far_other = lax.ppermute(far, AXES, between(0))
    scratch = [pltpu.VMEM(sums, F32)]
    mine, send = call(
        row_kernel, [(sums, F32), coded], [SM, VM, VM, VM], at, far, tiles, tiles_other, flops=flops, scratch=scratch
    )
    other = lax.ppermute(send, AXES, between(1))
    (part,) = call(
        col_kernel, [coded], [SM, VM, VM, VM, VM, VM, VM], at, far, far_other, mine, other, tiles, tiles_other,
        flops=flops, scratch=scratch,
    )
    got = exchange(part, 1, FIRST_Z[1])
    (part,) = call(sum_kernel, [((2, K, SEG), F32)], [VM], got)
    (out,) = call(total_kernel, [((K, SEG), F32)], [VM], lax.all_gather(part, "core", axis=0))
    return out


def solution(mesh):
    fine = Mesh(mesh.devices.reshape(SIZES), AXES)
    return jax.shard_map(
        per_device,
        mesh=fine,
        in_specs=(P(None, AXES), P(AXES, None, None), P(AXES), P(AXES)),
        out_specs=P(None, AXES),
        check_vma=False,
    )
```
